256 devices in a mesh: blk: 32 (over x_hi, z, core), tm: 8 (over x_lo, y).
Axes of the slice: x: 4 (x_hi: 2, x_lo: 2; x = x_hi * 2 + x_lo), y: 4, z: 8, core: 2. Of those that a mesh axis runs over, the one named last changes fastest.
Arguments:
- state_base: float32 [8, 5, 512, 32, 128], P('tm', None, 'blk')
- state_now: float32 [8, 5, 512, 32, 128], P('tm', None, 'blk')
- volume: float32 [512, 32, 128], P('blk'), may hold values from 0.5 to 2
- eddy_visc: float32 [512, 32, 128], P('blk'), may hold values from 0.05 to 0.5
- connect: int32 [32, 2, 3], replicated, may hold values from 0 to 31, as said below
- counts: int32 [32], replicated, may hold values from 8 to 16, as said below
Outputs:
- state_next: float32 [8, 5, 512, 32, 128], P('tm', None, 'blk')
The draws below stay inside these ranges and needn't reach their ends.
Inputs may be any that keep to these rules, and one draw needn't show every extreme that they name: `connect`: blocks form one closed circumferential cycle: the blocks named by a block's two faces are distinct from it; one of them lies exactly half the cycle away in block index, the other within 1 of half the cycle away or, where the cycle closes, next to it; the face, reversal and momentum signs are consistent on both sides of every shared face. `counts`: some block is full and some block is half full.
All inputs are finite; a program needn't handle non-finite values.
Results may differ from the reference program's by a relative error of at most 0.0003.
Values sent between devices are 32-bit elements; how exact they have to be, the bound alone decides.
No kernel may reach another device: no remote copies, remote signals or barrier semaphores. Data moves between devices by JAX's collectives and lax.ppermute only.
A program may use at most 128 MiB of HBM per device.

```python
import math
import jax
import jax.numpy as jnp
from jax import lax

NI = 16
NJ = 32
NK = 128
NT = 8
CELLS_I = 512
N_BLK = 32


def geometry(key):
    base_key = jax.random.fold_in(key, 7)
    key_flipi, key_flipk, key_count = jax.random.split(base_key, 3)
    half_cycle = N_BLK // 2
    block_ids = jnp.arange(N_BLK, dtype=jnp.int32)
    position = jnp.where(block_ids < half_cycle, 2 * block_ids, 2 * (block_ids - half_cycle) + 1).astype(jnp.int32)
    after_pos = jnp.mod(position + 1, N_BLK)
    before_pos = jnp.mod(position - 1, N_BLK)
    after_blk = (after_pos // 2 + jnp.mod(after_pos, 2) * half_cycle).astype(jnp.int32)
    before_blk = (before_pos // 2 + jnp.mod(before_pos, 2) * half_cycle).astype(jnp.int32)
    flip_i = jax.random.randint(key_flipi, (N_BLK,), 0, 2).astype(jnp.int32)
    flip_k = jax.random.randint(key_flipk, (N_BLK,), 0, 2).astype(jnp.int32)
    high_nbr = jnp.where(flip_i == 0, after_blk, before_blk)
    low_nbr = jnp.where(flip_i == 0, before_blk, after_blk)
    high_facing = jnp.where(flip_i == 0, flip_i[after_blk], 1 - flip_i[before_blk])
    low_facing = jnp.where(flip_i == 0, 1 - flip_i[before_blk], flip_i[after_blk])
    low_turn = jnp.bitwise_xor(flip_k, flip_k[low_nbr])
    high_turn = jnp.bitwise_xor(flip_k, flip_k[high_nbr])
    low_part = jnp.stack([low_nbr, low_facing, low_turn], axis=-1)
    high_part = jnp.stack([high_nbr, high_facing, high_turn], axis=-1)
    connect = jnp.stack([low_part, high_part], axis=1).astype(jnp.int32)
    counts = jax.random.randint(key_count, (N_BLK,), NI // 2, NI + 1).astype(jnp.int32)
    counts = counts.at[0].set(NI).at[1].set(NI // 2)
    return (connect, counts)


def draw_connect(key, part):
    return geometry(key)[0]


def draw_counts(key, part):
    return geometry(key)[1]


def make_state(key):
    shape = (NT, CELLS_I, NJ, NK)
    key_rho, key_vel, key_press = jax.random.split(key, 3)
    density = jnp.exp(jax.random.uniform(key_rho, shape, jnp.float32, jnp.log(0.6), jnp.log(1.6)))
    velocity = jnp.clip(0.3 * jax.random.normal(key_vel, (3,) + shape, jnp.float32), -0.9, 0.9)
    pressure = jnp.exp(jax.random.uniform(key_press, shape, jnp.float32, jnp.log(0.9), jnp.log(1.1)))
    momentum = density[None] * velocity
    energy = pressure / 0.4 + 0.5 * density * jnp.sum(velocity * velocity, axis=0)
    stacked = jnp.concatenate([density[None], momentum, energy[None]], axis=0)
    return jnp.moveaxis(stacked, 0, 1).astype(jnp.float32)


def draw_state_base(key, part):
    return make_state(jax.random.fold_in(key, 101))


def draw_state_now(key, part):
    return make_state(jax.random.fold_in(key, 202))


def levels(key, extent, pieces, least, top_value):
    def one(dim, shards_of):
        heights = jax.random.uniform(jax.random.fold_in(jax.random.fold_in(key, 6), dim), (shards_of,), jnp.float32, least / len(pieces), top_value / len(pieces))
        return jnp.repeat(jnp.exp(heights), extent[dim] // shards_of).reshape((-1,) + (1,) * (len(extent) - dim - 1))

    factor_of = one(*pieces[0])
    for cut in pieces[1:]:
        factor_of = factor_of * one(*cut)
    return factor_of


def setup_inputs(seed: int = 0) -> dict:
    seeds = jax.random.split(jax.random.key(seed), 7)
    return {
        "state_base": draw_state_base(jax.random.fold_in(seeds[6], 71), 0),
        "state_now": draw_state_now(jax.random.fold_in(seeds[6], 71), 0),
        "volume": jnp.clip(jnp.exp(math.log(2.0) - 1.3862944 * jax.random.uniform(seeds[2], (CELLS_I, NJ, NK), jnp.float32) ** levels(seeds[2], (CELLS_I, NJ, NK), ((0, 32),), -0.2, 0.2)), 0.5, 2.0),
        "eddy_visc": jnp.clip(jnp.exp(math.log(0.5) - 2.3025851 * jax.random.uniform(seeds[3], (CELLS_I, NJ, NK), jnp.float32) ** levels(seeds[3], (CELLS_I, NJ, NK), ((0, 32),), -0.2, 0.2)), 0.05, 0.5),
        "connect": draw_connect(jax.random.fold_in(seeds[6], 71), 0),
        "counts": draw_counts(jax.random.fold_in(seeds[6], 71), 0),
    }


GAMMA = 1.4
DISS_TWO = 0.5
DISS_FOUR = 1.0 / 32.0
COURANT = 2.0
SECTION_COEF = 0.5
NYQUIST = 4.0

def sliced(field, lower_edge, upper_edge, along):
    return lax.slice_in_dim(field, lower_edge, upper_edge, axis=along)

def primitives(field, direction):
    density = field[:, 0]
    momentum = field[:, 1:4]
    energy = field[:, 4]
    kinetic = 0.5 * lax.optimization_barrier(jnp.sum(momentum * momentum, axis=1)) / density
    pressure = (GAMMA - 1.0) * (energy - kinetic)
    sound_speed = jnp.sqrt(GAMMA * pressure / density)
    normal = field[:, 1 + direction] / density
    radius = jnp.abs(normal) + sound_speed
    fluxes = normal[:, None] * field
    fluxes = fluxes.at[:, 1 + direction].add(pressure)
    fluxes = fluxes.at[:, 4].add(pressure * normal)
    return (pressure, radius, fluxes)

def net_flux(field, viscous, direction):
    state_axis = 2 + direction
    press_axis = 1 + direction
    cell_count = field.shape[state_axis] - 4
    pressure, radius, fluxes = primitives(field, direction)
    second_diff = sliced(pressure, 2, cell_count + 4, press_axis) - 2.0 * sliced(pressure, 1, cell_count + 3, press_axis) + sliced(pressure, 0, cell_count + 2, press_axis)
    pressure_sum = sliced(pressure, 2, cell_count + 4, press_axis) + 2.0 * sliced(pressure, 1, cell_count + 3, press_axis) + sliced(pressure, 0, cell_count + 2, press_axis)
    sensor = jnp.abs(second_diff) / pressure_sum
    coef_two = DISS_TWO * jnp.maximum(sliced(sensor, 0, cell_count + 1, press_axis), sliced(sensor, 1, cell_count + 2, press_axis))
    coef_four = jnp.maximum(0.0, DISS_FOUR - coef_two)
    difference = sliced(field, 2, cell_count + 3, state_axis) - sliced(field, 1, cell_count + 2, state_axis)
    third_diff = sliced(field, 3, cell_count + 4, state_axis) - 3.0 * sliced(field, 2, cell_count + 3, state_axis) + 3.0 * sliced(field, 1, cell_count + 2, state_axis) - sliced(field, 0, cell_count + 1, state_axis)
    face_radius = 0.5 * (sliced(radius, 1, cell_count + 2, press_axis) + sliced(radius, 2, cell_count + 3, press_axis))
    central = 0.5 * (sliced(fluxes, 1, cell_count + 2, state_axis) + sliced(fluxes, 2, cell_count + 3, state_axis))
    face_visc = 0.5 * (sliced(viscous, 1, cell_count + 2, direction) + sliced(viscous, 2, cell_count + 3, direction))
    face_flux = central - face_radius[:, None] * (coef_two[:, None] * difference - coef_four[:, None] * third_diff) - face_visc[None, None] * difference
    return sliced(face_flux, 1, cell_count + 1, state_axis) - sliced(face_flux, 0, cell_count, state_axis)

def spectral_weight(time_lag):
    time_lag = jnp.mod(time_lag, NT)
    parity = 1.0 - 2.0 * jnp.mod(time_lag, 2).astype(jnp.float32)
    phase_angle = jnp.pi * jnp.where(time_lag == 0, 1, time_lag).astype(jnp.float32) / NT
    derivative = jnp.where(time_lag == 0, 0.0, -0.5 * parity * jnp.cos(phase_angle) / jnp.sin(phase_angle))
    return derivative + NYQUIST * parity / NT

def face_package(field, viscous, live_count):
    low_face = sliced(field, 0, 2, 2)
    high_face = jnp.flip(lax.dynamic_slice_in_dim(field, live_count - 2, 2, axis=2), axis=2)
    visc_low = sliced(viscous, 0, 2, 0)
    visc_high = jnp.flip(lax.dynamic_slice_in_dim(viscous, live_count - 2, 2, axis=0), axis=0)
    return (jnp.stack([low_face, high_face], axis=2), jnp.stack([visc_low, visc_high], axis=0))

def orient(layers, visc_layers, which_side, facing, reversal):
    normal_sign = jnp.where(facing == which_side, -1.0, 1.0)
    axial_sign = jnp.where(reversal == 1, -1.0, 1.0)
    turned = jnp.where(reversal == 1, jnp.flip(layers, axis=-1), layers)
    visc_turned = jnp.where(reversal == 1, jnp.flip(visc_layers, axis=-1), visc_layers)
    factors = jnp.ones((5,), jnp.float32).at[1].set(normal_sign).at[3].set(axial_sign)
    return (turned * factors[None, :, None, None, None], visc_turned)

def pseudo_section(state_base, field, own_volume, viscous, halo_low, halo_high, visc_low, visc_high, live_count, spectral):
    cell_count = field.shape[2]
    extended = jnp.concatenate([jnp.flip(halo_low, axis=2), field, sliced(field, cell_count - 2, cell_count, 2)], axis=2)
    extended = lax.dynamic_update_slice_in_dim(extended, halo_high, live_count + 2, axis=2)
    visc_extended = jnp.concatenate([jnp.flip(visc_low, axis=0), viscous, sliced(viscous, cell_count - 2, cell_count, 0)], axis=0)
    visc_extended = lax.dynamic_update_slice_in_dim(visc_extended, visc_high, live_count + 2, axis=0)
    residual = net_flux(extended, visc_extended, 0)
    radial_count = field.shape[3]
    wall_sign = jnp.ones((5,), jnp.float32).at[2].set(-1.0)[None, :, None, None, None]
    hub_ghost = jnp.flip(sliced(field, 0, 2, 3), axis=3) * wall_sign
    tip_ghost = jnp.flip(sliced(field, radial_count - 2, radial_count, 3), axis=3) * wall_sign
    radial = jnp.concatenate([hub_ghost, field, tip_ghost], axis=3)
    visc_radial = jnp.concatenate([jnp.flip(sliced(viscous, 0, 2, 1), axis=1), viscous, jnp.flip(sliced(viscous, radial_count - 2, radial_count, 1), axis=1)], axis=1)
    residual = residual + net_flux(radial, visc_radial, 1)
    axial_count = field.shape[4]
    inlet_cells = sliced(field, 0, 1, 4)
    outlet_cells = sliced(field, axial_count - 1, axial_count, 4)
    axial_ext = jnp.concatenate([inlet_cells, inlet_cells, field, outlet_cells, outlet_cells], axis=4)
    visc_inlet = sliced(viscous, 0, 1, 2)
    visc_outlet = sliced(viscous, axial_count - 1, axial_count, 2)
    visc_axial = jnp.concatenate([visc_inlet, visc_inlet, viscous, visc_outlet, visc_outlet], axis=2)
    residual = residual + net_flux(axial_ext, visc_axial, 2)
    density = field[:, 0]
    momentum = field[:, 1:4]
    kinetic = 0.5 * lax.optimization_barrier(jnp.sum(momentum * momentum, axis=1)) / density
    pressure = (GAMMA - 1.0) * (field[:, 4] - kinetic)
    sound_speed = jnp.sqrt(GAMMA * pressure / density)
    speeds = lax.optimization_barrier(jnp.sum(jnp.abs(momentum), axis=1)) / density + 3.0 * sound_speed
    denominator = speeds + own_volume[None] * (NT / 2.0)
    update = state_base - SECTION_COEF * COURANT * (residual + own_volume[None, None] * spectral) / denominator[:, None]
    alive_mask = jnp.arange(cell_count, dtype=jnp.int32) < live_count
    return jnp.where(alive_mask[None, None, :, None, None], update, 0.0)

def reference(state_base, state_now, volume, eddy_visc, connect, counts):
    time_index = jnp.arange(NT, dtype=jnp.int32)
    weights = spectral_weight(time_index[:, None] - time_index[None, :])

    def block_of(field, block_index, along):
        return lax.dynamic_slice_in_dim(field, (block_index * NI).astype(jnp.int32), NI, axis=along)

    def update_block(block_index):
        own_block = block_of(state_now, block_index, 2)
        own_base = block_of(state_base, block_index, 2)
        own_volume = block_of(volume, block_index, 0)
        own_visc = block_of(eddy_visc, block_index, 0)
        halo_list = []
        for which_side in (0, 1):
            neighbour = connect[block_index, which_side, 0]
            facing = connect[block_index, which_side, 1]
            reversal = connect[block_index, which_side, 2]
            package, visc_package = face_package(block_of(state_now, neighbour, 2), block_of(eddy_visc, neighbour, 0), counts[neighbour])
            layers = lax.dynamic_index_in_dim(package, facing, axis=2, keepdims=False)
            visc_layers = lax.dynamic_index_in_dim(visc_package, facing, axis=0, keepdims=False)
            halo_list.append(orient(layers, visc_layers, which_side, facing, reversal))
        spectral = jnp.dot(weights, own_block.reshape(NT, -1), precision=lax.Precision.HIGHEST).reshape(own_block.shape)
        return pseudo_section(own_base, own_block, own_volume, own_visc, halo_list[0][0], halo_list[1][0], halo_list[0][1], halo_list[1][1], counts[block_index], spectral)
    stacked = lax.map(update_block, jnp.arange(N_BLK, dtype=jnp.int32))
    return jnp.moveaxis(stacked, 0, 2).reshape(NT, 5, N_BLK * NI, NJ, NK)
```

```python
import functools

import jax
import jax.numpy as jnp
import numpy as np
from jax import lax
from jax.experimental import pallas as pl
from jax.experimental.pallas import tpu as pltpu
from jax.sharding import PartitionSpec as P

DISS_FOUR = 1.0 / 32.0
NYQUIST = 4.0
F32 = jnp.float32
HBM = pl.BlockSpec(memory_space=pltpu.HBM)
VMEM = pl.BlockSpec(memory_space=pltpu.VMEM)
SMEM = pl.BlockSpec(memory_space=pltpu.SMEM)


def spectral_weights(nt):
    time = np.arange(nt)
    lag = (time[:, None] - time[None, :]) % nt
    parity = 1.0 - 2.0 * (lag % 2)
    angle = np.pi * np.where(lag == 0, 1, lag) / nt
    derivative = np.where(lag == 0, 0.0, -0.5 * parity / np.tan(angle))
    weights = derivative + NYQUIST * parity / nt
    half = nt // 2
    near, far = weights[:half, :half], weights[:half, half:]
    return (0.5 * (near + far)).tolist(), (0.5 * (near - far)).tolist()


def half_side(connect, block, n_blk):
    half = lax.rem(block + n_blk // 2, n_blk)
    return jnp.where(connect[block, 0, 0] == half, 0, 1)


def spectral_kernel(even, odd, got_hbm, sent, got, made, arrived, left):
    nt, planes = got.shape[:2]
    half = nt // 2
    takes = [pltpu.make_async_copy(got_hbm.at[:, n], got.at[:, n], arrived.at[n]) for n in range(planes)]
    gives = [pltpu.make_async_copy(made.at[:, n], sent.at[:, n], left.at[n]) for n in range(planes)]
    for c in takes:
        c.start()
    for n in range(planes):
        takes[n].wait()
        states = [got[b, n] for b in range(nt)]
        sums = [states[b] + states[b + half] for b in range(half)]
        differences = [states[b] - states[b + half] for b in range(half)]
        for a in range(half):
            one = even[a][0] * sums[0]
            two = odd[a][0] * differences[0]
            for b in range(1, half):
                one += even[a][b] * sums[b]
                two += odd[a][b] * differences[b]
            made[a, n] = one + two
            made[a + half, n] = one - two
        gives[n].start()
    for c in gives:
        c.wait()


def final_kernel(kept_hbm, factor_hbm, source_hbm, out_hbm, kept, factor, source, out, arrived, left):
    nv, ni = kept.shape[:2]
    parts = 2
    size = ni // parts
    spots = [(v, pl.ds(h * size, size)) for h in range(parts) for v in range(nv)]
    takes = [
        [
            pltpu.make_async_copy(source_hbm.at[s], source.at[s], arrived.at[0, n]),
            pltpu.make_async_copy(kept_hbm.at[s], kept.at[s], arrived.at[1, n]),
        ]
        for n, s in enumerate(spots)
    ]
    for h in range(parts):
        part = pl.ds(h * size, size)
        takes[h * nv].append(pltpu.make_async_copy(factor_hbm.at[part], factor.at[part], arrived.at[2, h]))
    gives = [pltpu.make_async_copy(out.at[s], out_hbm.at[s], left.at[n]) for n, s in enumerate(spots)]
    for some in takes:
        for c in some:
            c.start()
    for n, s in enumerate(spots):
        for c in takes[n]:
            c.wait()
        out[s] = kept[s] - factor[s[1]] * source[s]
        gives[n].start()
    for c in gives:
        c.wait()


def sensor(before, here, after):
    return jnp.abs(after - 2.0 * here + before) / (after + 2.0 * here + before)


def coefs(nu_a, nu_b, lam_sum, visc_sum):
    e2 = 0.5 * jnp.maximum(nu_a, nu_b)
    e4 = jnp.maximum(0.0, DISS_FOUR - e2)
    lam = 0.5 * lam_sum
    return lam * e2 + 0.5 * visc_sum, lam * e4


def flux(v, d, state, speed, p):
    f = speed * state
    if v == 1 + d:
        f = f + p
    if v == 4:
        f = f + p * speed
    return f


def pressure(state, inv):
    rho, m1, m2, m3, energy = state
    return 0.4 * (energy - 0.5 * (m1 * m1 + m2 * m2 + m3 * m3) * inv)


def section_kernel(
    n_blk, nt, connect, counts, u_hbm, base_hbm, vol_hbm, visc_hbm, kept_hbm, inv_hbm, half_hbm, other_hbm,
    u, base, vol, visc, kept, inv_dens, pkg_half, pkg_other, arrived, left, layer_sems, pkg_sems,
):
    ni, nj, nk = vol.shape
    block = lax.axis_index("blk")
    live = counts[block]
    groups = arrived.shape[1]
    size = ni // groups

    def takes(g):
        part = pl.ds(g * size, size)
        pairs = ((u_hbm, u), (base_hbm, base), (vol_hbm, vol), (visc_hbm, visc))
        return [
            pltpu.make_async_copy(a.at[at], b.at[at], arrived.at[n, g])
            for n, (a, b) in enumerate(pairs)
            for at in [(slice(None), part) if len(a.shape) == 4 else part]
        ]

    def gives(g):
        part = pl.ds(g * size, size)
        return [
            pltpu.make_async_copy(kept.at[:, part], kept_hbm.at[:, part], left.at[0, g]),
            pltpu.make_async_copy(inv_dens.at[part], inv_hbm.at[part], left.at[1, g]),
        ]

    side = half_side(connect, block, n_blk)
    layers = []
    for pkg, face in ((pkg_half, side), (pkg_other, 1 - side)):
        for layer in (0, 1):
            cell = jnp.where(face == 0, layer, live - 1 - layer)
            layers.append(
                pltpu.make_async_copy(u_hbm.at[:, cell], pkg.at[pl.ds(0, 5), layer], layer_sems.at[len(layers)])
            )
            layers.append(pltpu.make_async_copy(visc_hbm.at[cell], pkg.at[5, layer], layer_sems.at[len(layers)]))
    for g in range(groups):
        for c in takes(g):
            c.start()
        if g == 0:
            for c in layers:
                c.start()
    for c in layers:
        c.wait()
    packages = [
        pltpu.make_async_copy(pkg_half, half_hbm, pkg_sems.at[0]),
        pltpu.make_async_copy(pkg_other, other_hbm, pkg_sems.at[1]),
    ]
    for c in packages:
        c.start()

    row = lax.broadcasted_iota(jnp.int32, (nj, nk), 0)
    col = lax.broadcasted_iota(jnp.int32, (nj, nk), 1)
    first_row, last_row = row == 0, row == nj - 1
    first_col, last_col = col == 0, col == nk - 1

    def up_j(x):
        return pltpu.roll(x, nj - 1, 0)

    def down_j(x):
        return pltpu.roll(x, 1, 0)

    def up_k(x):
        return pltpu.roll(x, nk - 1, 1)

    def down_k(x):
        return pltpu.roll(x, 1, 1)

    def plane(i, _):
        inv = 1.0 / u[0, i]
        p = pressure([u[v, i] for v in range(5)], inv)
        c = jnp.sqrt(1.4 * p * inv)
        mu = visc[i]
        speed_j, speed_k = u[2, i] * inv, u[3, i] * inv
        lam_i, lam_j, lam_k = jnp.abs(u[1, i] * inv) + c, jnp.abs(speed_j) + c, jnp.abs(speed_k) + c
        inv_den = 1.0 / (lam_i + lam_j + lam_k + vol[i] * (nt / 2.0))
        inv_dens[i] = inv_den
        nu_j = sensor(jnp.where(first_row, p, down_j(p)), p, jnp.where(last_row, p, up_j(p)))
        c2_j, c4_j = coefs(
            nu_j,
            jnp.where(last_row, nu_j, up_j(nu_j)),
            lam_j + jnp.where(last_row, lam_j, up_j(lam_j)),
            mu + jnp.where(last_row, mu, up_j(mu)),
        )
        nu_k = sensor(jnp.where(first_col, p, down_k(p)), p, jnp.where(last_col, p, up_k(p)))
        c2_k, c4_k = coefs(
            nu_k,
            jnp.where(last_col, 0.0, up_k(nu_k)),
            lam_k + jnp.where(last_col, lam_k, up_k(lam_k)),
            mu + jnp.where(last_col, mu, up_k(mu)),
        )
        wall_k = lam_k * jnp.maximum(0.0, DISS_FOUR - 0.5 * nu_k)
        for v in range(5):
            state = u[v, i]
            mirrored = -state if v == 2 else state
            d1 = jnp.where(last_row, mirrored, up_j(state)) - state
            d2 = d1 - jnp.where(first_row, 2.0 * state if v == 2 else 0.0, down_j(d1))
            d3 = jnp.where(last_row, -d2 if v == 2 else d2, up_j(d2)) - d2
            f = flux(v, 1, state, speed_j, p)
            face = 0.5 * (f + jnp.where(last_row, f if v == 2 else -f, up_j(f))) - c2_j * d1 + c4_j * d3
            wall = 0.0
            if v == 2:
                e2 = 0.5 * nu_j
                wall = f - (lam_j * e2 + mu) * (2.0 * state)
                wall = wall + lam_j * jnp.maximum(0.0, DISS_FOUR - e2) * (2.0 * d1 - 4.0 * state)
            total = face - jnp.where(first_row, wall, down_j(face))
            d1 = jnp.where(last_col, 0.0, up_k(state) - state)
            d2 = d1 - down_k(d1)
            d3 = jnp.where(last_col, 0.0, up_k(d2)) - d2
            f = flux(v, 2, state, speed_k, p)
            face = 0.5 * (f + jnp.where(last_col, f, up_k(f))) - c2_k * d1 + c4_k * d3
            total = total + face - jnp.where(first_col, f + wall_k * d1, down_k(face))
            kept[v, i] = base[v, i] - total * inv_den
        return 0

    def padding(i, _):
        inv_dens[i] = jnp.zeros((nj, nk), F32)
        for v in range(5):
            kept[v, i] = jnp.zeros((nj, nk), F32)
        return 0

    def group(g, _):
        for c in takes(g):
            c.wait()
        start, end = g * size, (g + 1) * size
        middle = jnp.clip(live, start, end)
        lax.fori_loop(start, middle, plane, 0)
        lax.fori_loop(middle, end, padding, 0)
        for c in gives(g):
            c.start()
        return 0

    lax.fori_loop(0, groups, group, 0)
    for g in range(groups):
        for c in gives(g):
            c.wait()
    for c in packages:
        c.wait()


def circumferential_kernel(
    n_blk, connect, counts, u, visc, vol_hbm, kept_hbm, inv_hbm, half_hbm, other_hbm, kept, factor,
    ext, vext, vol, kept_in, inv_dens, got_half, got_other, prs, rho_inv, snd, low, sems,
):
    nv, ni, nj, nk = u.shape
    block = lax.axis_index("blk")
    pairs = [(half_hbm, got_half), (other_hbm, got_other)]
    pairs += [(u.at[v], ext.at[v, pl.ds(2, ni)]) for v in range(nv)]
    pairs += [(visc, vext.at[pl.ds(2, ni)])]
    late = [(inv_hbm, inv_dens), (vol_hbm, vol)] + [(kept_hbm.at[v], kept_in.at[v]) for v in range(nv)]
    copies = [pltpu.make_async_copy(*pair, sems.at[n]) for n, pair in enumerate(pairs + late)]
    for c in copies:
        c.start()
    for c in copies[: len(pairs)]:
        c.wait()
    live = counts[block]
    side_of_half = half_side(connect, block, n_blk)
    turned = (nk - 1) - lax.broadcasted_iota(jnp.int32, (nj, nk), 1)

    def place(side, got):
        facing, reversal = connect[block, side, 1], connect[block, side, 2]
        sign_i = jnp.where(facing == side, -1.0, 1.0)
        sign_k = jnp.where(reversal == 1, -1.0, 1.0)

        def write(turn):
            for layer in (0, 1):
                at = 1 - layer if side == 0 else live + 2 + layer
                for v in range(6):
                    plane = got[v, layer]
                    if turn:
                        plane = jnp.take_along_axis(plane, turned, axis=1, mode="promise_in_bounds")
                    if v == 1:
                        plane = plane * sign_i
                    if v == 3:
                        plane = plane * sign_k
                    if v < 5:
                        ext[v, at] = plane
                    else:
                        vext[at] = plane

        pl.when(reversal == 1)(lambda: write(True))
        pl.when(reversal != 1)(lambda: write(False))

    @pl.when(side_of_half == 0)
    def _():
        place(0, got_half)
        place(1, got_other)

    @pl.when(side_of_half != 0)
    def _():
        place(1, got_half)
        place(0, got_other)

    def primitives(e, _):
        inv = 1.0 / ext[0, e]
        p = pressure([ext[v, e] for v in range(5)], inv)
        rho_inv[e] = inv
        prs[e] = p
        snd[e] = jnp.sqrt(1.4 * p * inv)
        return 0

    lax.fori_loop(0, live + 4, primitives, 0)

    def circ_face(e):
        p0, p1, p2, p3 = (prs[e + k] for k in (-1, 0, 1, 2))
        s1, s2 = ext[1, e] * rho_inv[e], ext[1, e + 1] * rho_inv[e + 1]
        lam_sum = (jnp.abs(s1) + snd[e]) + (jnp.abs(s2) + snd[e + 1])
        c2, c4 = coefs(sensor(p0, p1, p2), sensor(p1, p2, p3), lam_sum, vext[e] + vext[e + 1])
        for v in range(5):
            u0, u1, u2, u3 = (ext[v, e + k] for k in (-1, 0, 1, 2))
            d1 = u2 - u1
            d3 = (u3 - u2) - 2.0 * d1 + (u1 - u0)
            yield 0.5 * (flux(v, 0, u1, s1, p1) + flux(v, 0, u2, s2, p2)) - c2 * d1 + c4 * d3

    for v, f in enumerate(circ_face(1)):
        low[v] = f
    for c in copies[len(pairs) :]:
        c.wait()

    def plane(i, _):
        inv_den = inv_dens[i]
        factor[i] = vol[i] * inv_den
        for v, f in enumerate(circ_face(i + 2)):
            kept[v, i] = kept_in[v, i] - (f - low[v]) * inv_den
            low[v] = f
        return 0

    lax.fori_loop(0, live, plane, 0)

    def padding(i, _):
        factor[i] = jnp.zeros((nj, nk), F32)
        for v in range(5):
            kept[v, i] = jnp.zeros((nj, nk), F32)
        return 0

    lax.fori_loop(live, ni, padding, 0)


def local(n_blk, nt, state_base, state_now, volume, eddy_visc, connect, counts):
    u, base = state_now[0], state_base[0]
    nv, ni, nj, nk = u.shape
    state = jax.ShapeDtypeStruct(u.shape, F32)
    cells = jax.ShapeDtypeStruct(volume.shape, F32)
    package = jax.ShapeDtypeStruct((nv + 1, 2, nj, nk), F32)

    def vmem(x):
        return pltpu.VMEM(x.shape, x.dtype)

    params = pltpu.CompilerParams(vmem_limit_bytes=64 * 2**20)

    got = lax.all_to_all(u.reshape(nt, nv * ni // nt, nj, nk), "tm", 0, 0, tiled=True)

    groups = 4
    kept, inv_dens, pkg_half, pkg_other = pl.pallas_call(
        functools.partial(section_kernel, n_blk, nt),
        out_shape=[state, cells, package, package],
        in_specs=[SMEM, SMEM] + [HBM] * 4,
        out_specs=[HBM] * 4,
        scratch_shapes=[vmem(x) for x in (state, state, cells, cells, state, cells, package, package)]
        + [pltpu.SemaphoreType.DMA(n) for n in ((4, groups), (2, groups), (8,), (2,))],
        compiler_params=params,
        cost_estimate=pl.CostEstimate(flops=400 * u.size, bytes_accessed=16 * u.size, transcendentals=6 * volume.size),
        name="section",
    )(connect, counts, u, base, volume, eddy_visc)

    got, _ = lax.optimization_barrier((got, kept))

    half = n_blk // 2
    got_half = lax.ppermute(pkg_half, "blk", [(b, (b + half) % n_blk) for b in range(n_blk)])
    others = [(n_blk - 1 - b) if b in (0, n_blk - 1) else (b + half - 1) if b < half else (b - half + 1) for b in range(n_blk)]
    got_other = lax.ppermute(pkg_other, "blk", list(enumerate(others)))
    ids = jnp.arange(n_blk, dtype=jnp.int32)
    rest = jnp.where(
        (ids == 0) | (ids == n_blk - 1), n_blk - 1 - ids, jnp.where(ids < half, ids + half - 1, ids - half + 1)
    )
    halves = lax.rem(ids + half, n_blk)
    names = connect[:, :, 0]
    usual = jnp.all(
        ((names[:, 0] == halves) & (names[:, 1] == rest)) | ((names[:, 1] == halves) & (names[:, 0] == rest))
    )

    def by_ring(pkg, got_it):
        block = lax.axis_index("blk")
        there = connect[block, 1 - half_side(connect, block, n_blk), 0]

        def step(n, carry):
            moving, found = carry
            moving = lax.ppermute(moving, "blk", [(b, (b + 1) % n_blk) for b in range(n_blk)])
            return moving, jnp.where(lax.rem(block - n + n_blk, n_blk) == there, moving, found)

        return lax.fori_loop(1, n_blk, step, (pkg, got_it))[1]

    sent = pl.pallas_call(
        functools.partial(spectral_kernel, *spectral_weights(nt)),
        out_shape=jax.ShapeDtypeStruct(got.shape, F32),
        in_specs=[HBM],
        out_specs=HBM,
        scratch_shapes=[vmem(got)] * 2 + [pltpu.SemaphoreType.DMA((got.shape[1],))] * 2,
        compiler_params=params,
        cost_estimate=pl.CostEstimate(flops=2 * nt * u.size, bytes_accessed=8 * u.size, transcendentals=0),
        name="spectral",
    )(got)
    got_half, got_other, _ = lax.optimization_barrier((got_half, got_other, sent))
    got_other = lax.cond(usual, lambda pkg, got_it: got_it, by_ring, pkg_other, got_other)
    source = lax.all_to_all(sent, "tm", 0, 0, tiled=True)

    ghosted = jax.ShapeDtypeStruct((ni + 4, nj, nk), F32)
    kept, factor = pl.pallas_call(
        functools.partial(circumferential_kernel, n_blk),
        out_shape=[state, cells],
        in_specs=[SMEM, SMEM] + [HBM] * 7,
        out_specs=[VMEM, VMEM],
        scratch_shapes=[pltpu.VMEM((nv,) + ghosted.shape, F32)]
        + [vmem(x) for x in (ghosted, cells, state, cells, package, package, ghosted, ghosted, ghosted)]
        + [pltpu.VMEM((nv, nj, nk), F32), pltpu.SemaphoreType.DMA((2 * nv + 5,))],
        compiler_params=params,
        cost_estimate=pl.CostEstimate(flops=200000 * u.size, bytes_accessed=12 * u.size, transcendentals=2 * volume.size),
        name="circumferential",
    )(connect, counts, u, eddy_visc, volume, kept, inv_dens, got_half, got_other)

    out = pl.pallas_call(
        final_kernel,
        out_shape=state,
        in_specs=[HBM] * 3,
        out_specs=HBM,
        scratch_shapes=[vmem(x) for x in (state, cells, state, state)]
        + [pltpu.SemaphoreType.DMA(n) for n in ((3, 2 * nv), (2 * nv,))],
        compiler_params=params,
        name="final",
    )(kept, factor, source.reshape(u.shape))
    return out[None]


def solution(mesh):
    n_blk, nt = mesh.shape["blk"], mesh.shape["tm"]
    state, cells = P("tm", None, "blk", None, None), P("blk", None, None)
    return jax.shard_map(
        functools.partial(local, n_blk, nt),
        mesh=mesh,
        in_specs=(state, state, cells, cells, P(), P()),
        out_specs=state,
        check_vma=False,
    )
```

```python
import functools

import jax
import jax.numpy as jnp
import numpy as np
from jax import lax
from jax.experimental import pallas as pl
from jax.experimental.pallas import tpu as pltpu
from jax.sharding import PartitionSpec as P

DISS_FOUR = 1.0 / 32.0
NYQUIST = 4.0
F32 = jnp.float32
HBM = pl.BlockSpec(memory_space=pltpu.HBM)
VMEM = pl.BlockSpec(memory_space=pltpu.VMEM)
SMEM = pl.BlockSpec(memory_space=pltpu.SMEM)


def spectral_weights(nt):
    time = np.arange(nt)
    lag = (time[:, None] - time[None, :]) % nt
    parity = 1.0 - 2.0 * (lag % 2)
    angle = np.pi * np.where(lag == 0, 1, lag) / nt
    derivative = np.where(lag == 0, 0.0, -0.5 * parity / np.tan(angle))
    weights = derivative + NYQUIST * parity / nt
    half = nt // 2
    near, far = weights[:half, :half], weights[:half, half:]
    return (0.5 * (near + far)).tolist(), (0.5 * (near - far)).tolist()


def half_side(connect, block, n_blk):
    half = lax.rem(block + n_blk // 2, n_blk)
    return jnp.where(connect[block, 0, 0] == half, 0, 1)


def spectral_kernel(even, odd, got, sent, made, left):
    nt, planes = got.shape[:2]
    half = nt // 2
    gives = [pltpu.make_async_copy(made.at[:, n], sent.at[:, n], left.at[n]) for n in range(planes)]
    for n in range(planes):
        states = [got[b, n] for b in range(nt)]
        sums = [states[b] + states[b + half] for b in range(half)]
        differences = [states[b] - states[b + half] for b in range(half)]
        for a in range(half):
            one = even[a][0] * sums[0]
            two = odd[a][0] * differences[0]
            for b in range(1, half):
                one += even[a][b] * sums[b]
                two += odd[a][b] * differences[b]
            made[a, n] = one + two
            made[a + half, n] = one - two
        gives[n].start()
    for c in gives:
        c.wait()


def final_kernel(kept_hbm, factor_hbm, source_hbm, out_hbm, kept, factor, source, out, arrived, left):
    nv, ni = kept.shape[:2]
    parts = 2
    size = ni // parts
    spots = [(v, pl.ds(h * size, size)) for h in range(parts) for v in range(nv)]
    takes = [
        [
            pltpu.make_async_copy(source_hbm.at[s], source.at[s], arrived.at[0, n]),
            pltpu.make_async_copy(kept_hbm.at[s], kept.at[s], arrived.at[1, n]),
        ]
        for n, s in enumerate(spots)
    ]
    for h in range(parts):
        part = pl.ds(h * size, size)
        takes[h * nv].append(pltpu.make_async_copy(factor_hbm.at[part], factor.at[part], arrived.at[2, h]))
    gives = [pltpu.make_async_copy(out.at[s], out_hbm.at[s], left.at[n]) for n, s in enumerate(spots)]
    for some in takes:
        for c in some:
            c.start()
    for n, s in enumerate(spots):
        for c in takes[n]:
            c.wait()
        out[s] = kept[s] - factor[s[1]] * source[s]
        gives[n].start()
    for c in gives:
        c.wait()


def sensor(before, here, after):
    return jnp.abs(after - 2.0 * here + before) / (after + 2.0 * here + before)


def coefs(nu_a, nu_b, lam_sum, visc_sum):
    e2 = 0.5 * jnp.maximum(nu_a, nu_b)
    e4 = jnp.maximum(0.0, DISS_FOUR - e2)
    lam = 0.5 * lam_sum
    return lam * e2 + 0.5 * visc_sum, lam * e4


def flux(v, d, state, speed, p):
    f = speed * state
    if v == 1 + d:
        f = f + p
    if v == 4:
        f = f + p * speed
    return f


def pressure(state, inv):
    rho, m1, m2, m3, energy = state
    return 0.4 * (energy - 0.5 * (m1 * m1 + m2 * m2 + m3 * m3) * inv)


def section_kernel(
    n_blk, nt, connect, counts, u_hbm, base_hbm, vol_hbm, visc_hbm, kept_hbm, inv_hbm, half_hbm, other_hbm,
    u, base, vol, visc, kept, inv_dens, pkg_half, pkg_other, arrived, left, layer_sems, pkg_sems,
):
    ni, nj, nk = vol.shape
    block = lax.axis_index("blk")
    live = counts[block]
    groups = arrived.shape[1]
    size = ni // groups

    def takes(g):
        part = pl.ds(g * size, size)
        pairs = ((u_hbm, u), (base_hbm, base), (vol_hbm, vol), (visc_hbm, visc))
        return [
            pltpu.make_async_copy(a.at[at], b.at[at], arrived.at[n, g])
            for n, (a, b) in enumerate(pairs)
            for at in [(slice(None), part) if len(a.shape) == 4 else part]
        ]

    def gives(g):
        part = pl.ds(g * size, size)
        return [
            pltpu.make_async_copy(kept.at[:, part], kept_hbm.at[:, part], left.at[0, g]),
            pltpu.make_async_copy(inv_dens.at[part], inv_hbm.at[part], left.at[1, g]),
        ]

    side = half_side(connect, block, n_blk)
    layers = []
    for pkg, face in ((pkg_half, side), (pkg_other, 1 - side)):
        for layer in (0, 1):
            cell = jnp.where(face == 0, layer, live - 1 - layer)
            layers.append(
                pltpu.make_async_copy(u_hbm.at[:, cell], pkg.at[pl.ds(0, 5), layer], layer_sems.at[len(layers)])
            )
            layers.append(pltpu.make_async_copy(visc_hbm.at[cell], pkg.at[5, layer], layer_sems.at[len(layers)]))
    for g in range(groups):
        for c in takes(g):
            c.start()
        if g == 0:
            for c in layers:
                c.start()
    for c in layers:
        c.wait()
    packages = [
        pltpu.make_async_copy(pkg_half, half_hbm, pkg_sems.at[0]),
        pltpu.make_async_copy(pkg_other, other_hbm, pkg_sems.at[1]),
    ]
    for c in packages:
        c.start()

    row = lax.broadcasted_iota(jnp.int32, (nj, nk), 0)
    col = lax.broadcasted_iota(jnp.int32, (nj, nk), 1)
    first_row, last_row = row == 0, row == nj - 1
    first_col, last_col = col == 0, col == nk - 1

    def up_j(x):
        return pltpu.roll(x, nj - 1, 0)

    def down_j(x):
        return pltpu.roll(x, 1, 0)

    def up_k(x):
        return pltpu.roll(x, nk - 1, 1)

    def down_k(x):
        return pltpu.roll(x, 1, 1)

    def plane(i, _):
        inv = 1.0 / u[0, i]
        p = pressure([u[v, i] for v in range(5)], inv)
        c = jnp.sqrt(1.4 * p * inv)
        mu = visc[i]
        speed_j, speed_k = u[2, i] * inv, u[3, i] * inv
        lam_i, lam_j, lam_k = jnp.abs(u[1, i] * inv) + c, jnp.abs(speed_j) + c, jnp.abs(speed_k) + c
        inv_den = 1.0 / (lam_i + lam_j + lam_k + vol[i] * (nt / 2.0))
        inv_dens[i] = inv_den
        nu_j = sensor(jnp.where(first_row, p, down_j(p)), p, jnp.where(last_row, p, up_j(p)))
        c2_j, c4_j = coefs(
            nu_j,
            jnp.where(last_row, nu_j, up_j(nu_j)),
            lam_j + jnp.where(last_row, lam_j, up_j(lam_j)),
            mu + jnp.where(last_row, mu, up_j(mu)),
        )
        nu_k = sensor(jnp.where(first_col, p, down_k(p)), p, jnp.where(last_col, p, up_k(p)))
        c2_k, c4_k = coefs(
            nu_k,
            jnp.where(last_col, 0.0, up_k(nu_k)),
            lam_k + jnp.where(last_col, lam_k, up_k(lam_k)),
            mu + jnp.where(last_col, mu, up_k(mu)),
        )
        wall_k = lam_k * jnp.maximum(0.0, DISS_FOUR - 0.5 * nu_k)
        for v in range(5):
            state = u[v, i]
            mirrored = -state if v == 2 else state
            d1 = jnp.where(last_row, mirrored, up_j(state)) - state
            d2 = d1 - jnp.where(first_row, 2.0 * state if v == 2 else 0.0, down_j(d1))
            d3 = jnp.where(last_row, -d2 if v == 2 else d2, up_j(d2)) - d2
            f = flux(v, 1, state, speed_j, p)
            face = 0.5 * (f + jnp.where(last_row, f if v == 2 else -f, up_j(f))) - c2_j * d1 + c4_j * d3
            wall = 0.0
            if v == 2:
                e2 = 0.5 * nu_j
                wall = f - (lam_j * e2 + mu) * (2.0 * state)
                wall = wall + lam_j * jnp.maximum(0.0, DISS_FOUR - e2) * (2.0 * d1 - 4.0 * state)
            total = face - jnp.where(first_row, wall, down_j(face))
            d1 = jnp.where(last_col, 0.0, up_k(state) - state)
            d2 = d1 - down_k(d1)
            d3 = jnp.where(last_col, 0.0, up_k(d2)) - d2
            f = flux(v, 2, state, speed_k, p)
            face = 0.5 * (f + jnp.where(last_col, f, up_k(f))) - c2_k * d1 + c4_k * d3
            total = total + face - jnp.where(first_col, f + wall_k * d1, down_k(face))
            kept[v, i] = base[v, i] - total * inv_den
        return 0

    def padding(i, _):
        inv_dens[i] = jnp.zeros((nj, nk), F32)
        for v in range(5):
            kept[v, i] = jnp.zeros((nj, nk), F32)
        return 0

    def group(g, _):
        for c in takes(g):
            c.wait()
        start, end = g * size, (g + 1) * size
        middle = jnp.clip(live, start, end)
        lax.fori_loop(start, middle, plane, 0)
        lax.fori_loop(middle, end, padding, 0)
        for c in gives(g):
            c.start()
        return 0

    lax.fori_loop(0, groups, group, 0)
    for g in range(groups):
        for c in gives(g):
            c.wait()
    for c in packages:
        c.wait()


def circumferential_kernel(
    n_blk, connect, counts, u, visc, vol_hbm, kept_hbm, inv_hbm, half_hbm, other_hbm, kept, factor,
    ext, vext, vol, kept_in, inv_dens, got_half, got_other, prs, rho_inv, snd, low, sems,
):
    nv, ni, nj, nk = u.shape
    block = lax.axis_index("blk")
    pairs = [(half_hbm, got_half), (other_hbm, got_other)]
    pairs += [(u.at[v], ext.at[v, pl.ds(2, ni)]) for v in range(nv)]
    pairs += [(visc, vext.at[pl.ds(2, ni)])]
    late = [(inv_hbm, inv_dens), (vol_hbm, vol)] + [(kept_hbm.at[v], kept_in.at[v]) for v in range(nv)]
    copies = [pltpu.make_async_copy(*pair, sems.at[n]) for n, pair in enumerate(pairs + late)]
    for c in copies:
        c.start()
    for c in copies[: len(pairs)]:
        c.wait()
    live = counts[block]
    side_of_half = half_side(connect, block, n_blk)
    turned = (nk - 1) - lax.broadcasted_iota(jnp.int32, (nj, nk), 1)

    def place(side, got):
        facing, reversal = connect[block, side, 1], connect[block, side, 2]
        sign_i = jnp.where(facing == side, -1.0, 1.0)
        sign_k = jnp.where(reversal == 1, -1.0, 1.0)

        def write(turn):
            for layer in (0, 1):
                at = 1 - layer if side == 0 else live + 2 + layer
                for v in range(6):
                    plane = got[v, layer]
                    if turn:
                        plane = jnp.take_along_axis(plane, turned, axis=1, mode="promise_in_bounds")
                    if v == 1:
                        plane = plane * sign_i
                    if v == 3:
                        plane = plane * sign_k
                    if v < 5:
                        ext[v, at] = plane
                    else:
                        vext[at] = plane

        pl.when(reversal == 1)(lambda: write(True))
        pl.when(reversal != 1)(lambda: write(False))

    @pl.when(side_of_half == 0)
    def _():
        place(0, got_half)
        place(1, got_other)

    @pl.when(side_of_half != 0)
    def _():
        place(1, got_half)
        place(0, got_other)

    def primitives(e, _):
        inv = 1.0 / ext[0, e]
        p = pressure([ext[v, e] for v in range(5)], inv)
        rho_inv[e] = inv
        prs[e] = p
        snd[e] = jnp.sqrt(1.4 * p * inv)
        return 0

    lax.fori_loop(0, live + 4, primitives, 0)

    def circ_face(e):
        p0, p1, p2, p3 = (prs[e + k] for k in (-1, 0, 1, 2))
        s1, s2 = ext[1, e] * rho_inv[e], ext[1, e + 1] * rho_inv[e + 1]
        lam_sum = (jnp.abs(s1) + snd[e]) + (jnp.abs(s2) + snd[e + 1])
        c2, c4 = coefs(sensor(p0, p1, p2), sensor(p1, p2, p3), lam_sum, vext[e] + vext[e + 1])
        for v in range(5):
            u0, u1, u2, u3 = (ext[v, e + k] for k in (-1, 0, 1, 2))
            d1 = u2 - u1
            d3 = (u3 - u2) - 2.0 * d1 + (u1 - u0)
            yield 0.5 * (flux(v, 0, u1, s1, p1) + flux(v, 0, u2, s2, p2)) - c2 * d1 + c4 * d3

    for v, f in enumerate(circ_face(1)):
        low[v] = f
    for c in copies[len(pairs) :]:
        c.wait()

    def plane(i, _):
        inv_den = inv_dens[i]
        factor[i] = vol[i] * inv_den
        for v, f in enumerate(circ_face(i + 2)):
            kept[v, i] = kept_in[v, i] - (f - low[v]) * inv_den
            low[v] = f
        return 0

    lax.fori_loop(0, live, plane, 0)

    def padding(i, _):
        factor[i] = jnp.zeros((nj, nk), F32)
        for v in range(5):
            kept[v, i] = jnp.zeros((nj, nk), F32)
        return 0

    lax.fori_loop(live, ni, padding, 0)


def local(n_blk, nt, state_base, state_now, volume, eddy_visc, connect, counts):
    u, base = state_now[0], state_base[0]
    nv, ni, nj, nk = u.shape
    state = jax.ShapeDtypeStruct(u.shape, F32)
    cells = jax.ShapeDtypeStruct(volume.shape, F32)
    package = jax.ShapeDtypeStruct((nv + 1, 2, nj, nk), F32)

    def vmem(x):
        return pltpu.VMEM(x.shape, x.dtype)


    got = lax.all_to_all(u.reshape(nt, nv * ni // nt, nj, nk), "tm", 0, 0, tiled=True)

    groups = 4
    kept, inv_dens, pkg_half, pkg_other = pl.pallas_call(
        functools.partial(section_kernel, n_blk, nt),
        out_shape=[state, cells, package, package],
        in_specs=[SMEM, SMEM] + [HBM] * 4,
        out_specs=[HBM] * 4,
        scratch_shapes=[vmem(x) for x in (state, state, cells, cells, state, cells, package, package)]
        + [pltpu.SemaphoreType.DMA(n) for n in ((4, groups), (2, groups), (8,), (2,))],
        compiler_params=pltpu.CompilerParams(vmem_limit_bytes=62 * 2**20),
        cost_estimate=pl.CostEstimate(flops=400 * u.size, bytes_accessed=16 * u.size, transcendentals=6 * volume.size),
        name="section",
    )(connect, counts, u, base, volume, eddy_visc)

    got, _ = lax.optimization_barrier((got, kept))

    half = n_blk // 2
    got_half = lax.ppermute(pkg_half, "blk", [(b, (b + half) % n_blk) for b in range(n_blk)])
    others = [(n_blk - 1 - b) if b in (0, n_blk - 1) else (b + half - 1) if b < half else (b - half + 1) for b in range(n_blk)]
    got_other = lax.ppermute(pkg_other, "blk", list(enumerate(others)))
    ids = jnp.arange(n_blk, dtype=jnp.int32)
    rest = jnp.where(
        (ids == 0) | (ids == n_blk - 1), n_blk - 1 - ids, jnp.where(ids < half, ids + half - 1, ids - half + 1)
    )
    halves = lax.rem(ids + half, n_blk)
    names = connect[:, :, 0]
    usual = jnp.all(
        ((names[:, 0] == halves) & (names[:, 1] == rest)) | ((names[:, 1] == halves) & (names[:, 0] == rest))
    )

    def by_ring(pkg, got_it):
        block = lax.axis_index("blk")
        there = connect[block, 1 - half_side(connect, block, n_blk), 0]

        def step(n, carry):
            moving, found = carry
            moving = lax.ppermute(moving, "blk", [(b, (b + 1) % n_blk) for b in range(n_blk)])
            return moving, jnp.where(lax.rem(block - n + n_blk, n_blk) == there, moving, found)

        return lax.fori_loop(1, n_blk, step, (pkg, got_it))[1]

    sent = pl.pallas_call(
        functools.partial(spectral_kernel, *spectral_weights(nt)),
        out_shape=jax.ShapeDtypeStruct(got.shape, F32),
        in_specs=[VMEM],
        out_specs=HBM,
        scratch_shapes=[vmem(got), pltpu.SemaphoreType.DMA((got.shape[1],))],
        compiler_params=pltpu.CompilerParams(vmem_limit_bytes=8 * 2**20),
        cost_estimate=pl.CostEstimate(flops=2 * nt * u.size, bytes_accessed=8 * u.size, transcendentals=0),
        name="spectral",
    )(got)
    got_half, got_other, _ = lax.optimization_barrier((got_half, got_other, sent))
    got_other = lax.cond(usual, lambda pkg, got_it: got_it, by_ring, pkg_other, got_other)
    source = lax.all_to_all(sent, "tm", 0, 0, tiled=True)

    ghosted = jax.ShapeDtypeStruct((ni + 4, nj, nk), F32)
    kept, factor = pl.pallas_call(
        functools.partial(circumferential_kernel, n_blk),
        out_shape=[state, cells],
        in_specs=[SMEM, SMEM] + [HBM] * 7,
        out_specs=[VMEM, VMEM],
        scratch_shapes=[pltpu.VMEM((nv,) + ghosted.shape, F32)]
        + [vmem(x) for x in (ghosted, cells, state, cells, package, package, ghosted, ghosted, ghosted)]
        + [pltpu.VMEM((nv, nj, nk), F32), pltpu.SemaphoreType.DMA((2 * nv + 5,))],
        compiler_params=pltpu.CompilerParams(vmem_limit_bytes=64 * 2**20),
        cost_estimate=pl.CostEstimate(flops=200000 * u.size, bytes_accessed=12 * u.size, transcendentals=2 * volume.size),
        name="circumferential",
    )(connect, counts, u, eddy_visc, volume, kept, inv_dens, got_half, got_other)

    out = pl.pallas_call(
        final_kernel,
        out_shape=state,
        in_specs=[HBM] * 3,
        out_specs=HBM,
        scratch_shapes=[vmem(x) for x in (state, cells, state, state)]
        + [pltpu.SemaphoreType.DMA(n) for n in ((3, 2 * nv), (2 * nv,))],
        compiler_params=pltpu.CompilerParams(vmem_limit_bytes=64 * 2**20),
        name="final",
    )(kept, factor, source.reshape(u.shape))
    return out[None]


def solution(mesh):
    n_blk, nt = mesh.shape["blk"], mesh.shape["tm"]
    state, cells = P("tm", None, "blk", None, None), P("blk", None, None)
    return jax.shard_map(
        functools.partial(local, n_blk, nt),
        mesh=mesh,
        in_specs=(state, state, cells, cells, P(), P()),
        out_specs=state,
        check_vma=False,
    )
```

```python
import functools

import jax
import jax.numpy as jnp
import numpy as np
from jax import lax
from jax.experimental import pallas as pl
from jax.experimental.pallas import tpu as pltpu
from jax.sharding import PartitionSpec as P

DISS_FOUR = 1.0 / 32.0
NYQUIST = 4.0
F32 = jnp.float32
HBM = pl.BlockSpec(memory_space=pltpu.HBM)
VMEM = pl.BlockSpec(memory_space=pltpu.VMEM)
SMEM = pl.BlockSpec(memory_space=pltpu.SMEM)


def spectral_weights(nt):
    time = np.arange(nt)
    lag = (time[:, None] - time[None, :]) % nt
    parity = 1.0 - 2.0 * (lag % 2)
    angle = np.pi * np.where(lag == 0, 1, lag) / nt
    derivative = np.where(lag == 0, 0.0, -0.5 * parity / np.tan(angle))
    weights = derivative + NYQUIST * parity / nt
    half = nt // 2
    near, far = weights[:half, :half], weights[:half, half:]
    return (0.5 * (near + far)).tolist(), (0.5 * (near - far)).tolist()


def half_side(connect, block, n_blk):
    half = lax.rem(block + n_blk // 2, n_blk)
    return jnp.where(connect[block, 0, 0] == half, 0, 1)


def spectral_kernel(even, odd, got, sent, made, left):
    nt, planes = got.shape[:2]
    half = nt // 2
    groups = left.shape[0]
    size = planes // groups
    parts = [pl.ds(g * size, size) for g in range(groups)]
    gives = [pltpu.make_async_copy(made.at[:, part], sent.at[:, part], left.at[g]) for g, part in enumerate(parts)]
    for n in range(planes):
        states = [got[b, n] for b in range(nt)]
        sums = [states[b] + states[b + half] for b in range(half)]
        differences = [states[b] - states[b + half] for b in range(half)]
        for a in range(half):
            one = even[a][0] * sums[0]
            two = odd[a][0] * differences[0]
            for b in range(1, half):
                one += even[a][b] * sums[b]
                two += odd[a][b] * differences[b]
            made[a, n] = one + two
            made[a + half, n] = one - two
        if n % size == size - 1:
            gives[n // size].start()
    for c in gives:
        c.wait()


def final_kernel(kept, factor, source_hbm, out_hbm, source, out, arrived, left):
    nv = kept.shape[0]
    takes = [pltpu.make_async_copy(source_hbm.at[v], source.at[v], arrived.at[v]) for v in range(nv)]
    gives = [pltpu.make_async_copy(out.at[v], out_hbm.at[v], left.at[v]) for v in range(nv)]
    for c in takes:
        c.start()
    for v in range(nv):
        takes[v].wait()
        out[v] = kept[v] - factor[...] * source[v]
        gives[v].start()
    for c in gives:
        c.wait()


def factor_kernel(vol, inv_dens, factor):
    factor[...] = vol[...] * inv_dens[...]


def sensor(before, here, after):
    return jnp.abs(after - 2.0 * here + before) / (after + 2.0 * here + before)


def coefs(nu_a, nu_b, lam_sum, visc_sum):
    e2 = 0.5 * jnp.maximum(nu_a, nu_b)
    e4 = jnp.maximum(0.0, DISS_FOUR - e2)
    lam = 0.5 * lam_sum
    return lam * e2 + 0.5 * visc_sum, lam * e4


def flux(v, d, state, speed, p):
    f = speed * state
    if v == 1 + d:
        f = f + p
    if v == 4:
        f = f + p * speed
    return f


def pressure(state, inv):
    rho, m1, m2, m3, energy = state
    return 0.4 * (energy - 0.5 * (m1 * m1 + m2 * m2 + m3 * m3) * inv)


def section_kernel(
    n_blk, nt, connect, counts, u_hbm, base_hbm, vol_hbm, visc_hbm, kept_hbm, inv_hbm, half_hbm, other_hbm,
    u, base, vol, visc, kept, inv_dens, pkg_half, pkg_other, arrived, left, layer_sems, pkg_sems,
):
    ni, nj, nk = vol.shape
    block = lax.axis_index("blk")
    live = counts[block]
    groups = arrived.shape[1]
    size = ni // groups

    def takes(g):
        part = pl.ds(g * size, size)
        pairs = ((u_hbm, u), (base_hbm, base), (vol_hbm, vol), (visc_hbm, visc))
        return [
            pltpu.make_async_copy(a.at[at], b.at[at], arrived.at[n, g])
            for n, (a, b) in enumerate(pairs)
            for at in [(slice(None), part) if len(a.shape) == 4 else part]
        ]

    def gives(g):
        part = pl.ds(g * size, size)
        return [
            pltpu.make_async_copy(kept.at[:, part], kept_hbm.at[:, part], left.at[0, g]),
            pltpu.make_async_copy(inv_dens.at[part], inv_hbm.at[part], left.at[1, g]),
        ]

    side = half_side(connect, block, n_blk)
    layers = []
    for pkg, face in ((pkg_half, side), (pkg_other, 1 - side)):
        for layer in (0, 1):
            cell = jnp.where(face == 0, layer, live - 1 - layer)
            layers.append(
                pltpu.make_async_copy(u_hbm.at[:, cell], pkg.at[pl.ds(0, 5), layer], layer_sems.at[len(layers)])
            )
            layers.append(pltpu.make_async_copy(visc_hbm.at[cell], pkg.at[5, layer], layer_sems.at[len(layers)]))
    for g in range(groups):
        for c in takes(g):
            c.start()
        if g == 0:
            for c in layers:
                c.start()
    for c in layers:
        c.wait()
    packages = [
        pltpu.make_async_copy(pkg_half, half_hbm, pkg_sems.at[0]),
        pltpu.make_async_copy(pkg_other, other_hbm, pkg_sems.at[1]),
    ]
    for c in packages:
        c.start()

    row = lax.broadcasted_iota(jnp.int32, (nj, nk), 0)
    col = lax.broadcasted_iota(jnp.int32, (nj, nk), 1)
    first_row, last_row = row == 0, row == nj - 1
    first_col, last_col = col == 0, col == nk - 1

    def up_j(x):
        return pltpu.roll(x, nj - 1, 0)

    def down_j(x):
        return pltpu.roll(x, 1, 0)

    def up_k(x):
        return pltpu.roll(x, nk - 1, 1)

    def down_k(x):
        return pltpu.roll(x, 1, 1)

    def plane(i, _):
        inv = 1.0 / u[0, i]
        p = pressure([u[v, i] for v in range(5)], inv)
        c = jnp.sqrt(1.4 * p * inv)
        mu = visc[i]
        speed_j, speed_k = u[2, i] * inv, u[3, i] * inv
        lam_i, lam_j, lam_k = jnp.abs(u[1, i] * inv) + c, jnp.abs(speed_j) + c, jnp.abs(speed_k) + c
        inv_den = 1.0 / (lam_i + lam_j + lam_k + vol[i] * (nt / 2.0))
        inv_dens[i] = inv_den
        nu_j = sensor(jnp.where(first_row, p, down_j(p)), p, jnp.where(last_row, p, up_j(p)))
        c2_j, c4_j = coefs(
            nu_j,
            jnp.where(last_row, nu_j, up_j(nu_j)),
            lam_j + jnp.where(last_row, lam_j, up_j(lam_j)),
            mu + jnp.where(last_row, mu, up_j(mu)),
        )
        nu_k = sensor(jnp.where(first_col, p, down_k(p)), p, jnp.where(last_col, p, up_k(p)))
        c2_k, c4_k = coefs(
            nu_k,
            jnp.where(last_col, 0.0, up_k(nu_k)),
            lam_k + jnp.where(last_col, lam_k, up_k(lam_k)),
            mu + jnp.where(last_col, mu, up_k(mu)),
        )
        wall_k = lam_k * jnp.maximum(0.0, DISS_FOUR - 0.5 * nu_k)
        for v in range(5):
            state = u[v, i]
            mirrored = -state if v == 2 else state
            d1 = jnp.where(last_row, mirrored, up_j(state)) - state
            d2 = d1 - jnp.where(first_row, 2.0 * state if v == 2 else 0.0, down_j(d1))
            d3 = jnp.where(last_row, -d2 if v == 2 else d2, up_j(d2)) - d2
            f = flux(v, 1, state, speed_j, p)
            face = 0.5 * (f + jnp.where(last_row, f if v == 2 else -f, up_j(f))) - c2_j * d1 + c4_j * d3
            wall = 0.0
            if v == 2:
                e2 = 0.5 * nu_j
                wall = f - (lam_j * e2 + mu) * (2.0 * state)
                wall = wall + lam_j * jnp.maximum(0.0, DISS_FOUR - e2) * (2.0 * d1 - 4.0 * state)
            total = face - jnp.where(first_row, wall, down_j(face))
            d1 = jnp.where(last_col, 0.0, up_k(state) - state)
            d2 = d1 - down_k(d1)
            d3 = jnp.where(last_col, 0.0, up_k(d2)) - d2
            f = flux(v, 2, state, speed_k, p)
            face = 0.5 * (f + jnp.where(last_col, f, up_k(f))) - c2_k * d1 + c4_k * d3
            total = total + face - jnp.where(first_col, f + wall_k * d1, down_k(face))
            kept[v, i] = base[v, i] - total * inv_den
        return 0

    def padding(i, _):
        inv_dens[i] = jnp.zeros((nj, nk), F32)
        for v in range(5):
            kept[v, i] = jnp.zeros((nj, nk), F32)
        return 0

    def group(g, _):
        for c in takes(g):
            c.wait()
        start, end = g * size, (g + 1) * size
        middle = jnp.clip(live, start, end)
        lax.fori_loop(start, middle, plane, 0)
        lax.fori_loop(middle, end, padding, 0)
        for c in gives(g):
            c.start()
        return 0

    lax.fori_loop(0, groups, group, 0)
    for g in range(groups):
        for c in gives(g):
            c.wait()
    for c in packages:
        c.wait()


def circumferential_kernel(
    n_blk, connect, counts, u, visc, kept_hbm, inv_hbm, half_hbm, other_hbm, kept,
    ext, vext, kept_in, inv_dens, got_half, got_other, prs, rho_inv, snd, low, sems,
):
    nv, ni, nj, nk = u.shape
    block = lax.axis_index("blk")
    pairs = [(half_hbm, got_half), (other_hbm, got_other)]
    pairs += [(u.at[v], ext.at[v, pl.ds(2, ni)]) for v in range(nv)]
    pairs += [(visc, vext.at[pl.ds(2, ni)])]
    late = [(inv_hbm, inv_dens)] + [(kept_hbm.at[v], kept_in.at[v]) for v in range(nv)]
    copies = [pltpu.make_async_copy(*pair, sems.at[n]) for n, pair in enumerate(pairs + late)]
    for c in copies:
        c.start()
    for c in copies[: len(pairs)]:
        c.wait()
    live = counts[block]
    side_of_half = half_side(connect, block, n_blk)
    turned = (nk - 1) - lax.broadcasted_iota(jnp.int32, (nj, nk), 1)

    def place(side, got):
        facing, reversal = connect[block, side, 1], connect[block, side, 2]
        sign_i = jnp.where(facing == side, -1.0, 1.0)
        sign_k = jnp.where(reversal == 1, -1.0, 1.0)

        def write(turn):
            for layer in (0, 1):
                at = 1 - layer if side == 0 else live + 2 + layer
                for v in range(6):
                    plane = got[v, layer]
                    if turn:
                        plane = jnp.take_along_axis(plane, turned, axis=1, mode="promise_in_bounds")
                    if v == 1:
                        plane = plane * sign_i
                    if v == 3:
                        plane = plane * sign_k
                    if v < 5:
                        ext[v, at] = plane
                    else:
                        vext[at] = plane

        pl.when(reversal == 1)(lambda: write(True))
        pl.when(reversal != 1)(lambda: write(False))

    @pl.when(side_of_half == 0)
    def _():
        place(0, got_half)
        place(1, got_other)

    @pl.when(side_of_half != 0)
    def _():
        place(1, got_half)
        place(0, got_other)

    def primitives(e, _):
        inv = 1.0 / ext[0, e]
        p = pressure([ext[v, e] for v in range(5)], inv)
        rho_inv[e] = inv
        prs[e] = p
        snd[e] = jnp.sqrt(1.4 * p * inv)
        return 0

    lax.fori_loop(0, live + 4, primitives, 0)

    def circ_face(e):
        p0, p1, p2, p3 = (prs[e + k] for k in (-1, 0, 1, 2))
        s1, s2 = ext[1, e] * rho_inv[e], ext[1, e + 1] * rho_inv[e + 1]
        lam_sum = (jnp.abs(s1) + snd[e]) + (jnp.abs(s2) + snd[e + 1])
        c2, c4 = coefs(sensor(p0, p1, p2), sensor(p1, p2, p3), lam_sum, vext[e] + vext[e + 1])
        for v in range(5):
            u0, u1, u2, u3 = (ext[v, e + k] for k in (-1, 0, 1, 2))
            d1 = u2 - u1
            d3 = (u3 - u2) - 2.0 * d1 + (u1 - u0)
            yield 0.5 * (flux(v, 0, u1, s1, p1) + flux(v, 0, u2, s2, p2)) - c2 * d1 + c4 * d3

    for v, f in enumerate(circ_face(1)):
        low[v] = f
    for c in copies[len(pairs) :]:
        c.wait()

    def plane(i, _):
        inv_den = inv_dens[i]
        for v, f in enumerate(circ_face(i + 2)):
            kept[v, i] = kept_in[v, i] - (f - low[v]) * inv_den
            low[v] = f
        return 0

    lax.fori_loop(0, live, plane, 0)

    def padding(i, _):
        for v in range(5):
            kept[v, i] = jnp.zeros((nj, nk), F32)
        return 0

    lax.fori_loop(live, ni, padding, 0)


def local(n_blk, nt, state_base, state_now, volume, eddy_visc, connect, counts):
    u, base = state_now[0], state_base[0]
    nv, ni, nj, nk = u.shape
    state = jax.ShapeDtypeStruct(u.shape, F32)
    cells = jax.ShapeDtypeStruct(volume.shape, F32)
    package = jax.ShapeDtypeStruct((nv + 1, 2, nj, nk), F32)

    def vmem(x):
        return pltpu.VMEM(x.shape, x.dtype)


    got = lax.all_to_all(u.reshape(nt, nv * ni // nt, nj, nk), "tm", 0, 0, tiled=True)

    groups = 4
    kept, inv_dens, pkg_half, pkg_other = pl.pallas_call(
        functools.partial(section_kernel, n_blk, nt),
        out_shape=[state, cells, package, package],
        in_specs=[SMEM, SMEM] + [HBM] * 4,
        out_specs=[HBM] * 4,
        scratch_shapes=[vmem(x) for x in (state, state, cells, cells, state, cells, package, package)]
        + [pltpu.SemaphoreType.DMA(n) for n in ((4, groups), (2, groups), (8,), (2,))],
        compiler_params=pltpu.CompilerParams(vmem_limit_bytes=62 * 2**20),
        cost_estimate=pl.CostEstimate(flops=400 * u.size, bytes_accessed=16 * u.size, transcendentals=6 * volume.size),
        name="section",
    )(connect, counts, u, base, volume, eddy_visc)

    got, _ = lax.optimization_barrier((got, kept))

    half = n_blk // 2
    got_half = lax.ppermute(pkg_half, "blk", [(b, (b + half) % n_blk) for b in range(n_blk)])
    others = [(n_blk - 1 - b) if b in (0, n_blk - 1) else (b + half - 1) if b < half else (b - half + 1) for b in range(n_blk)]
    got_other = lax.ppermute(pkg_other, "blk", list(enumerate(others)))
    ids = jnp.arange(n_blk, dtype=jnp.int32)
    rest = jnp.where(
        (ids == 0) | (ids == n_blk - 1), n_blk - 1 - ids, jnp.where(ids < half, ids + half - 1, ids - half + 1)
    )
    halves = lax.rem(ids + half, n_blk)
    names = connect[:, :, 0]
    usual = jnp.all(
        ((names[:, 0] == halves) & (names[:, 1] == rest)) | ((names[:, 1] == halves) & (names[:, 0] == rest))
    )

    def by_ring(pkg, got_it):
        block = lax.axis_index("blk")
        there = connect[block, 1 - half_side(connect, block, n_blk), 0]

        def step(n, carry):
            moving, found = carry
            moving = lax.ppermute(moving, "blk", [(b, (b + 1) % n_blk) for b in range(n_blk)])
            return moving, jnp.where(lax.rem(block - n + n_blk, n_blk) == there, moving, found)

        return lax.fori_loop(1, n_blk, step, (pkg, got_it))[1]

    sent = pl.pallas_call(
        functools.partial(spectral_kernel, *spectral_weights(nt)),
        out_shape=jax.ShapeDtypeStruct(got.shape, F32),
        in_specs=[VMEM],
        out_specs=HBM,
        scratch_shapes=[vmem(got), pltpu.SemaphoreType.DMA((nv,))],
        compiler_params=pltpu.CompilerParams(vmem_limit_bytes=8 * 2**20),
        cost_estimate=pl.CostEstimate(flops=2 * nt * u.size, bytes_accessed=8 * u.size, transcendentals=0),
        name="spectral",
    )(got)
    got_half, got_other, _ = lax.optimization_barrier((got_half, got_other, sent))
    got_other = lax.cond(usual, lambda pkg, got_it: got_it, by_ring, pkg_other, got_other)
    source = lax.all_to_all(sent, "tm", 0, 0, tiled=True)

    factor = pl.pallas_call(
        factor_kernel,
        out_shape=cells,
        in_specs=[VMEM] * 2,
        out_specs=VMEM,
        compiler_params=pltpu.CompilerParams(vmem_limit_bytes=64 * 2**20),
        name="factor",
    )(volume, lax.optimization_barrier((inv_dens, sent))[0])
    kept, factor = lax.optimization_barrier((kept, factor))

    ghosted = jax.ShapeDtypeStruct((ni + 4, nj, nk), F32)
    kept = pl.pallas_call(
        functools.partial(circumferential_kernel, n_blk),
        out_shape=state,
        in_specs=[SMEM, SMEM] + [HBM] * 6,
        out_specs=VMEM,
        scratch_shapes=[pltpu.VMEM((nv,) + ghosted.shape, F32)]
        + [vmem(x) for x in (ghosted, state, cells, package, package, ghosted, ghosted, ghosted)]
        + [pltpu.VMEM((nv, nj, nk), F32), pltpu.SemaphoreType.DMA((2 * nv + 4,))],
        compiler_params=pltpu.CompilerParams(vmem_limit_bytes=40 * 2**20),
        cost_estimate=pl.CostEstimate(flops=200000 * u.size, bytes_accessed=12 * u.size, transcendentals=2 * volume.size),
        name="circumferential",
    )(connect, counts, u, eddy_visc, kept, inv_dens, got_half, got_other)

    out = pl.pallas_call(
        final_kernel,
        out_shape=state,
        in_specs=[VMEM, VMEM, HBM],
        out_specs=HBM,
        scratch_shapes=[vmem(state)] * 2 + [pltpu.SemaphoreType.DMA((nv,))] * 2,
        compiler_params=pltpu.CompilerParams(vmem_limit_bytes=8 * 2**20),
        name="final",
    )(kept, factor, source.reshape(u.shape))
    return out[None]


def solution(mesh):
    n_blk, nt = mesh.shape["blk"], mesh.shape["tm"]
    state, cells = P("tm", None, "blk", None, None), P("blk", None, None)
    return jax.shard_map(
        functools.partial(local, n_blk, nt),
        mesh=mesh,
        in_specs=(state, state, cells, cells, P(), P()),
        out_specs=state,
        check_vma=False,
    )
```
